256 devices in a mesh: replica: 8 (over y, core), fsdp: 32 (over x, z).
Axes of the slice: x: 4, y: 4, z: 8, core: 2. Of those that a mesh axis runs over, the one named last changes fastest.
Arguments:
- gradients: bfloat16 [8, 4096, 8192], P('replica', 'fsdp'), may hold values from -6 to 6
- left_factor: float32 [32, 1, 8, 512, 512], P('fsdp', None, None, 'replica'), may hold values from -6 to 6
- right_factor: float32 [32, 1, 8, 512, 512], P('fsdp', None, None, 'replica'), may hold values from -6 to 6
- left_root: bfloat16 [32, 1, 8, 512, 512], P('fsdp', None, None, 'replica'), may hold values from -0.25 to 0.25
- right_root: bfloat16 [32, 1, 8, 512, 512], P('fsdp'), may hold values from -0.25 to 0.25
- owner_table: int32 [8, 16], replicated, may hold values from 0 to 31, as said below
Outputs:
- left_next: float32 [32, 1, 8, 512, 512], P('fsdp', None, None, 'replica')
- right_next: float32 [32, 1, 8, 512, 512], P('fsdp', None, None, 'replica')
- update: bfloat16 [32, 1, 8, 512, 512], P('fsdp', None, None, 'replica')
The draws below stay inside these ranges and needn't reach their ends.
Inputs may be any that keep to these rules, and one draw needn't show every extreme that they name: In each row of owner_table no owner is named more than 1 times.
All inputs are finite; a program needn't handle non-finite values.
Results may differ from the reference program's by a relative error of at most 0.02.
Values may be sent and summed in bfloat16 or wider, within the bound.
No kernel may reach another device: no remote copies, remote signals or barrier semaphores. Data moves between devices by JAX's collectives and lax.ppermute only.
A program may use at most 64 MiB of HBM per device.

```python
import jax
import jax.numpy as jnp
from jax import lax

COLS = 8192
BS = 512
ROWS = 4096
MOST = 1
N_REPLICA = 8
N_FSDP = 32


def draw_gradients(key, part):
    key = jax.random.fold_in(key, 11)
    noise_key, row_key, col_key = jax.random.split(key, 3)
    row_part = jax.random.truncated_normal(row_key, -3.0, 3.0, (ROWS,), jnp.float32)
    col_part = jax.random.truncated_normal(col_key, -3.0, 3.0, (COLS,), jnp.float32)
    noise = 0.35 * jax.random.truncated_normal(noise_key, -6.0, 6.0, (N_REPLICA, ROWS, COLS), jnp.float32)
    strength = 1.2
    shared = strength / N_REPLICA * row_part[:, None] * col_part[None, :]
    return (noise + shared[None, :, :]).astype(jnp.bfloat16)


def draw_owner_table(key, part):
    key = jax.random.fold_in(key, 7)
    first, second, third = jax.random.split(key, 3)
    block_rows = ROWS // BS
    block_cols = COLS // BS
    owners = N_FSDP
    depth = MOST
    contender_list = owners * depth
    preferred_pick = jax.random.permutation(first, owners) < max(1, owners // 8)
    block_owner_lookup = jnp.arange(contender_list, dtype=jnp.int32) // depth
    extra_credit = jnp.where(preferred_pick[block_owner_lookup], 2 ** 17, 0).astype(jnp.int32)
    random_jitter = jax.random.randint(second, (block_rows, contender_list), 0, 2 ** 16, dtype=jnp.int32)
    ranking_values = (random_jitter + extra_credit[None, :]) * contender_list + jnp.arange(contender_list, dtype=jnp.int32)[None, :]
    unused, chosen = lax.top_k(ranking_values, block_cols)
    picked = block_owner_lookup[chosen]
    shuffle = jax.random.randint(third, (block_rows, block_cols), 0, 2 ** 16, dtype=jnp.int32) * block_cols + jnp.arange(block_cols, dtype=jnp.int32)[None, :]
    ordering = jnp.argsort(shuffle, axis=1)
    return jnp.take_along_axis(picked, ordering, axis=1).astype(jnp.int32)


def block_levels(stream_key, shape, pieces, smallest, high):
    def one(dim, parts):
        heights = jax.random.uniform(jax.random.fold_in(jax.random.fold_in(stream_key, 6), dim), (parts,), jnp.float32, smallest / len(pieces), high / len(pieces))
        return jnp.repeat(jnp.exp(heights), shape[dim] // parts).reshape((-1,) + (1,) * (len(shape) - dim - 1))

    level = one(*pieces[0])
    for cut in pieces[1:]:
        level = level * one(*cut)
    return level


def bell_draw(own_key, extent, deviation, bound, shards=(), kind=jnp.bfloat16):
    array = jax.random.normal(own_key, extent, jnp.float32) * deviation
    if len(shards) > 0:
        array = block_levels(own_key, extent, shards, -0.22, 0.18) * array
    return jnp.clip(array, min=-bound, max=bound).astype(kind)


def setup_inputs(seed: int = 0) -> dict:
    keys = jax.random.split(jax.random.key(seed), 7)
    gradients = draw_gradients(jax.random.fold_in(keys[6], 71), 0)
    left_factor = bell_draw(keys[1], (N_FSDP, MOST, ROWS // BS, BS, BS), 0.5, 6.0, ((0, 32), (3, 8)), jnp.float32)
    right_factor = bell_draw(keys[2], (N_FSDP, MOST, ROWS // BS, BS, BS), 0.5, 6.0, ((0, 32), (3, 8)), jnp.float32)
    left_root = bell_draw(keys[3], (N_FSDP, MOST, ROWS // BS, BS, BS), BS ** -0.5, 0.25, ((0, 32), (3, 8)))
    right_root = bell_draw(keys[4], (N_FSDP, MOST, ROWS // BS, BS, BS), BS ** -0.5, 0.25, ((0, 32),))
    owner_table = draw_owner_table(jax.random.fold_in(keys[6], 71), 0)
    return dict(gradients=gradients, left_factor=left_factor, right_factor=right_factor, left_root=left_root, right_root=right_root, owner_table=owner_table)


decay_rate = 0.9


def slot_table(owner_table, owner_count, slot_depth):
    block_cols = owner_table.shape[1]
    owner_match = (owner_table[:, :, None] == jnp.arange(owner_count, dtype=jnp.int32)[None, None, :]).astype(jnp.int32)
    earlier = (jnp.cumsum(owner_match, axis=1) - owner_match).astype(jnp.int32)
    column_rank = jnp.sum(earlier * owner_match, axis=2).astype(jnp.int32)
    slot_match = (column_rank[:, :, None] == jnp.arange(slot_depth, dtype=jnp.int32)[None, None, :]).astype(jnp.int32)
    joint = owner_match[:, :, None, :] * slot_match[:, :, :, None]
    column_ids = jnp.arange(block_cols, dtype=jnp.int32)[None, :, None, None]
    col_table = jnp.sum(joint * column_ids, axis=1).astype(jnp.int32)
    col_valid = jnp.sum(joint, axis=1).astype(jnp.int32)
    return col_table, col_valid


def reference(gradients, left_factor, right_factor, left_root, right_root, owner_table):
    summed = jnp.sum(gradients.astype(jnp.float32), axis=0).astype(jnp.bfloat16)
    block_rows = ROWS // BS
    block_cols = COLS // BS
    tiles = summed.reshape(block_rows, BS, block_cols, BS).transpose(0, 2, 1, 3)
    col_table, col_valid = slot_table(owner_table, N_FSDP, MOST)
    row_ids = jnp.arange(block_rows, dtype=jnp.int32)[:, None]
    scale = (1.0 - decay_rate) / BS

    def per_owner(items):
        owner, left_one, single_right_factor, lroot_one, rroot_one = items
        picks = jnp.take(col_table, owner, axis=2)
        live = jnp.take(col_valid, owner, axis=2)
        chosen = tiles[row_ids, picks]
        chosen = chosen * live[:, :, None, None].astype(jnp.bfloat16)
        chosen = jnp.transpose(chosen, (1, 0, 2, 3)).astype(jnp.float32)
        stat_left = jnp.einsum('kjab,kjcb->kjac', chosen, chosen)
        stat_right = jnp.einsum('kjba,kjbc->kjac', chosen, chosen)
        left_new = decay_rate * left_one + scale * stat_left
        right_new = decay_rate * single_right_factor + scale * stat_right
        half = jnp.einsum('kjab,kjbc->kjac', lroot_one.astype(jnp.float32), chosen).astype(jnp.bfloat16)
        result = jnp.einsum('kjab,kjbc->kjac', half.astype(jnp.float32), rroot_one.astype(jnp.float32)).astype(jnp.bfloat16)
        return left_new, right_new, result

    owners = jnp.arange(N_FSDP, dtype=jnp.int32)
    left_next, right_next, update = lax.map(per_owner, (owners, left_factor, right_factor, left_root, right_root))
    return (left_next, right_next, update)
```

```python
import functools

import jax
import jax.numpy as jnp
from jax import lax
from jax.experimental import pallas as pl
from jax.experimental.pallas import tpu as pltpu
from jax.sharding import PartitionSpec as P

decay_rate = 0.9
MIB = 1 << 20


def y_shift(d):
    return [(r, (r + 2 * d) % 8) for r in range(8)]


core_swap = [(r, r ^ 1) for r in range(8)]


def permute(x, pairs):
    return lax.ppermute(x, "replica", pairs)


def pair_sum_kernel(idx, *refs):
    mine, other, outs = refs[:4], refs[4:8], refs[8:]
    for a, b, o in zip(mine, other, outs):
        o[...] = (a[0].astype(jnp.float32) + b[0].astype(jnp.float32)).astype(o.dtype)


def pair_sum(idx, own, recv):
    groups, rows, cols = own.shape
    step = cols // 4

    def pick(k):
        return lambda t, s: (2 * lax.rem(s[0] // 2 + k, 4) + lax.rem(s[0], 2), 0, t)

    specs = [pl.BlockSpec((1, rows, step), pick(k)) for k in range(4)]
    return pl.pallas_call(
        pair_sum_kernel,
        grid_spec=pltpu.PrefetchScalarGridSpec(
            num_scalar_prefetch=1,
            grid=(cols // step,),
            in_specs=specs + specs,
            out_specs=[pl.BlockSpec((rows, step), lambda t, s: (0, t))] * 4,
        ),
        out_shape=[jax.ShapeDtypeStruct((rows, cols), own.dtype)] * 4,
        compiler_params=pltpu.CompilerParams(vmem_limit_bytes=16 * MIB),
        cost_estimate=pl.CostEstimate(flops=rows * cols * 4, bytes_accessed=24 * rows * cols, transcendentals=0),
        name="pair_sum",
    )(idx, *([own] * 4), *([recv] * 4))


def place_kernel(idx, table, a, b, c, d, out):
    block = out.shape[-1]
    my_row = idx[1] // 4
    out[...] = jnp.zeros_like(out)
    for col in range(a.shape[-1] // block):
        cut = slice(col * block, (col + 1) * block)
        total = (
            a[:, cut].astype(jnp.float32)
            + b[:, cut].astype(jnp.float32)
            + c[:, cut].astype(jnp.float32)
            + d[:, cut].astype(jnp.float32)
        )
        out[table[my_row, col]] = total.astype(out.dtype)


def place(idx, table, parts, owners, block):
    rows, cols = parts[0].shape
    return pl.pallas_call(
        place_kernel,
        grid_spec=pltpu.PrefetchScalarGridSpec(
            num_scalar_prefetch=2,
            grid=(1,),
            in_specs=[pl.BlockSpec((rows, cols), lambda t, s, w: (0, 0))] * 4,
            out_specs=pl.BlockSpec((owners, rows, block), lambda t, s, w: (0, 0, 0)),
        ),
        out_shape=jax.ShapeDtypeStruct((owners, rows, block), parts[0].dtype),
        compiler_params=pltpu.CompilerParams(vmem_limit_bytes=16 * MIB),
        cost_estimate=pl.CostEstimate(flops=rows * cols * 4, bytes_accessed=12 * rows * cols, transcendentals=0),
        name="place",
    )(idx, table, *parts)


def update_kernel(idx, *refs):
    low, high = refs[:8], refs[8:16]
    left, right, lroot, rroot, left_out, right_out, out, whole = refs[16:]
    j = pl.program_id(0)
    r = idx[0]
    y, core = r // 2, lax.rem(r, 2)

    def assemble(pieces):
        for c in range(2):
            for k, d in enumerate((0, 3, 1, 2)):
                row = 2 * lax.rem(y + d, 4) + (core if c == 0 else 1 - core)
                for q in range(4):
                    start = pl.multiple_of(q * 128 + row * 16, 16)
                    whole[pl.ds(start, 16), :] = pieces[4 * c + k][q]

    @pl.when(j < 4)
    def _():
        assemble(low)

    @pl.when(j >= 4)
    def _():
        assemble(high)

    scale = (1.0 - decay_rate) / whole.shape[0]
    share = left.shape[1]
    mine = whole[pl.ds(pl.multiple_of(r * share, share), share), :]
    stat_left = lax.dot_general(mine, whole[...], (((1,), (1,)), ((), ())), preferred_element_type=jnp.float32)
    left_out[0] = decay_rate * left[0] + scale * stat_left
    cols = whole[:, pl.ds(pl.multiple_of(y * 2 * share, 2 * share), 2 * share)]
    stat_right = lax.dot_general(cols, whole[...], (((0,), (0,)), ((), ())), preferred_element_type=jnp.float32)
    stat_right = jnp.where(core == 0, stat_right[:share], stat_right[share:])
    right_out[0] = decay_rate * right[0] + scale * stat_right
    half = jnp.dot(lroot[0], whole[...], preferred_element_type=jnp.float32).astype(jnp.bfloat16)
    out[0] = jnp.dot(half, rroot[0], preferred_element_type=jnp.float32).astype(out.dtype)


def update(idx, low, high, left, right, lroot, rroot):
    blocks, share, size = left.shape
    piece_low = pl.BlockSpec((4, 16, size), lambda j, s: (jnp.minimum(j, 3), 0, 0))
    piece_high = pl.BlockSpec((4, 16, size), lambda j, s: (jnp.maximum(j - 4, 0), 0, 0))
    thin = pl.BlockSpec((1, share, size), lambda j, s: (j, 0, 0))
    full = pl.BlockSpec((1, size, size), lambda j, s: (j, 0, 0))
    return pl.pallas_call(
        update_kernel,
        grid_spec=pltpu.PrefetchScalarGridSpec(
            num_scalar_prefetch=1,
            grid=(blocks,),
            in_specs=[piece_low] * 8 + [piece_high] * 8 + [thin, thin, thin, full],
            out_specs=[thin, thin, thin],
            scratch_shapes=[pltpu.VMEM((size, size), jnp.bfloat16)],
        ),
        out_shape=[
            jax.ShapeDtypeStruct(left.shape, left.dtype),
            jax.ShapeDtypeStruct(right.shape, right.dtype),
            jax.ShapeDtypeStruct(lroot.shape, lroot.dtype),
        ],
        compiler_params=pltpu.CompilerParams(vmem_limit_bytes=32 * MIB),
        cost_estimate=pl.CostEstimate(flops=blocks * 8 * share * size * size, bytes_accessed=14 * MIB, transcendentals=0),
        name="update",
    )(idx, *low, *high, left, right, lroot, rroot)


def shards(gradients, left_factor, right_factor, left_root, right_root, owner_table):
    owners = lax.axis_size("fsdp")
    block_size = left_factor.shape[-1]
    _, row_count, col_count = gradients.shape
    idx = jnp.stack([lax.axis_index("replica"), lax.axis_index("fsdp")]).astype(jnp.int32)

    swapped = permute(gradients, core_swap)
    grouped = (8, row_count // 8, col_count)
    kept, to_next, to_far, to_prev = pair_sum(idx, gradients.reshape(grouped), swapped.reshape(grouped))
    parts = [kept, permute(to_next, y_shift(1)), permute(to_far, y_shift(2)), permute(to_prev, y_shift(-1))]
    outgoing = place(idx, owner_table, parts, owners, block_size)
    received = lax.all_to_all(outgoing, "fsdp", split_axis=0, concat_axis=0, tiled=True)

    low, high = received[: owners // 2], received[owners // 2 :]
    low_prev = permute(low, y_shift(1))
    high_next = permute(high, y_shift(-1))
    high_prev = permute(high, y_shift(1))
    low_next = permute(low, y_shift(-1))
    low_far = permute(low_prev, y_shift(1))
    high_far = permute(high_next, y_shift(-1))
    low_pieces = [low, low_prev, low_next, low_far]
    high_pieces = [high, high_prev, high_next, high_far]
    low_pieces += [permute(p, core_swap) for p in low_pieces]
    high_pieces += [permute(p, core_swap) for p in high_pieces]

    left_new, right_new, result = update(
        idx, low_pieces, high_pieces, left_factor[0, 0], right_factor[0, 0], left_root[0, 0], right_root[0, 0]
    )
    return (left_new[None, None], right_new[None, None], result[None, None])


def solution(mesh):
    placed = (
        P("replica", "fsdp", None),
        P("fsdp", None, None, "replica", None),
        P("fsdp", None, None, "replica", None),
        P("fsdp", None, None, "replica", None),
        P("fsdp", None, None, None, None),
        P(),
    )
    return jax.shard_map(
        shards,
        mesh=mesh,
        in_specs=placed,
        out_specs=(
            P("fsdp", None, None, "replica", None),
            P("fsdp", None, None, "replica", None),
            P("fsdp", None, None, "replica", None),
        ),
        check_vma=False,
    )
```

```python
import jax
import jax.numpy as jnp
from jax import lax
from jax.experimental import pallas as pl
from jax.experimental.pallas import tpu as pltpu
from jax.sharding import PartitionSpec as P

decay_rate = 0.9
MIB = 1 << 20
SPLIT = 4
VMEM = pl.BlockSpec(memory_space=pltpu.VMEM)
SMEM = pl.BlockSpec(memory_space=pltpu.SMEM)
HBM = pl.BlockSpec(memory_space=pltpu.HBM)

core_swap = [(r, r ^ 1) for r in range(8)]
split_ring = [(r, (r + 2 - 4 * (r % 2)) % 8) for r in range(8)]


def y_shift(d):
    return [(r, (r + 2 * d) % 8) for r in range(8)]


def permute(x, pairs):
    return lax.ppermute(x, "replica", pairs)


def group_of(r, k):
    return 2 * lax.rem(r // 2 + k, 4) + lax.rem(r, 2)


def own_rows_kernel(grads, out, sems):
    copies = [pltpu.make_async_copy(grads.at[group_of(lax.axis_index("replica"), k)], out.at[k], sems.at[k]) for k in range(4)]
    for c in copies:
        c.start()
    for c in copies:
        c.wait()


def own_rows(grads):
    _, rows, cols = grads.shape
    return pl.pallas_call(
        own_rows_kernel,
        in_specs=[HBM],
        out_specs=VMEM,
        out_shape=jax.ShapeDtypeStruct((4, rows, cols), grads.dtype),
        scratch_shapes=[pltpu.SemaphoreType.DMA((4,))],
        compiler_params=pltpu.CompilerParams(vmem_limit_bytes=8 * MIB),
        cost_estimate=pl.CostEstimate(flops=0, bytes_accessed=4 * MIB, transcendentals=0),
        name="own_rows",
    )(grads)


def pair_sum_kernel(own, recv, *outs):
    for k in range(4):
        total = own[k].astype(jnp.float32) + recv[group_of(lax.axis_index("replica"), k)].astype(jnp.float32)
        outs[k][...] = total.astype(own.dtype)


def pair_sum(own, recv, block):
    _, rows, cols = own.shape
    return pl.pallas_call(
        pair_sum_kernel,
        in_specs=[VMEM, VMEM],
        out_specs=[VMEM] * 4,
        out_shape=[jax.ShapeDtypeStruct((rows, cols), own.dtype)] * 4,
        compiler_params=pltpu.CompilerParams(vmem_limit_bytes=8 * MIB),
        cost_estimate=pl.CostEstimate(flops=4 * rows * cols, bytes_accessed=4 * MIB, transcendentals=0),
        name="pair_sum",
    )(own, recv)


def place_kernel(table, *refs):
    halves = len(refs) // 5
    my_row = lax.axis_index("fsdp") // 4
    for h in range(halves):
        a, b, c, d = refs[4 * h : 4 * h + 4]
        out = refs[4 * halves + h]
        width = out.shape[-1]
        out[...] = jnp.zeros_like(out)
        for col in range(a.shape[-1] // width):
            cut = slice(col * width, (col + 1) * width)
            total = (
                a[:, cut].astype(jnp.float32)
                + b[:, cut].astype(jnp.float32)
                + c[:, cut].astype(jnp.float32)
                + d[:, cut].astype(jnp.float32)
            )
            out[table[my_row, col]] = total.astype(out.dtype)


def place(table, parts, owners, width):
    rows, cols = parts[0].shape
    halves = len(parts) // 4
    return pl.pallas_call(
        place_kernel,
        in_specs=[SMEM] + [VMEM] * len(parts),
        out_specs=[VMEM] * halves,
        out_shape=[jax.ShapeDtypeStruct((owners, rows, width), parts[0].dtype)] * halves,
        compiler_params=pltpu.CompilerParams(vmem_limit_bytes=8 * MIB),
        cost_estimate=pl.CostEstimate(flops=4 * rows * cols * halves, bytes_accessed=MIB * halves, transcendentals=0),
        name="place",
    )(table, *parts)


def update_kernel(first, *refs):
    pieces, (left, right, lroot, rroot) = refs[: len(places)], refs[len(places) : len(places) + 4]
    left_out, right_out, out, whole, left_new, right_new, result, sems = refs[-8:]
    r = lax.axis_index("replica")
    y, core = r // 2, lax.rem(r, 2)
    count, share, size = left_new.shape
    quarter = size // 4
    scale = (1.0 - decay_rate) / size
    sends = []
    for n in range(count):
        j = first + n
        block = whole.at[n]
        for piece, (ahead, dy, flip) in zip(pieces, places):
            row = 2 * lax.rem(y + dy + ahead * (2 * core - 1) + 4, 4) + (1 - core if flip else core)
            for q in range(4):
                start = pl.multiple_of(q * quarter + row * 16, 16)
                block[pl.ds(start, 16), :] = piece[4 * n + q]
        mine = block[pl.ds(pl.multiple_of(r * share, share), share), :]
        stat_left = lax.dot_general(mine, block[...], (((1,), (1,)), ((), ())), preferred_element_type=jnp.float32)
        left_new[n] = decay_rate * left[j] + scale * stat_left
        turned = block[:, pl.ds(pl.multiple_of(y * 2 * share, 2 * share), 2 * share)].T
        turned = jnp.where(core == 0, turned[:share], turned[share:])
        both = jnp.dot(jnp.concatenate([turned, lroot[j]], axis=0), block[...], preferred_element_type=jnp.float32)
        right_new[n] = decay_rate * right[j] + scale * both[:share]
        half = both[share:].astype(jnp.bfloat16)
        result[n] = jnp.dot(half, rroot[j], preferred_element_type=jnp.float32).astype(result.dtype)
        for m, (src, dst) in enumerate(((left_new, left_out), (right_new, right_out), (result, out))):
            sends.append(pltpu.make_async_copy(src.at[n], dst.at[j], sems.at[m, n]))
            sends[-1].start()
    for send in sends:
        send.wait()


def update(first, count, pieces, left, right, lroot, rroot, earlier):
    _, share, size = left.shape
    shapes = [jax.ShapeDtypeStruct(x.shape, x.dtype) for x in (left, right, lroot)]
    return pl.pallas_call(
        lambda *refs: update_kernel(first, *refs),
        in_specs=[VMEM] * (len(pieces) + 4) + [HBM] * len(earlier),
        out_specs=[HBM] * 3,
        out_shape=shapes,
        scratch_shapes=[pltpu.VMEM((count, size, size), lroot.dtype)]
        + [pltpu.VMEM((count, share, size), x.dtype) for x in shapes]
        + [pltpu.SemaphoreType.DMA((3, count))],
        input_output_aliases={len(pieces) + 4 + n: n for n in range(len(earlier))},
        compiler_params=pltpu.CompilerParams(vmem_limit_bytes=16 * MIB),
        cost_estimate=pl.CostEstimate(flops=count * 8 * share * size * size, bytes_accessed=2 * count * MIB, transcendentals=0),
        name="update",
    )(*pieces, left, right, lroot, rroot, *earlier)


def tie(*xs):
    return lax.optimization_barrier(xs)


def cross(x):
    return permute(x, core_swap)


def gather(own, split):
    parts = [own[: 4 * split], own[4 * split :]]
    groups = []
    for n, part in enumerate(parts):
        a, b = tie(part, cross(part))
        near, near_other = permute(a, split_ring), permute(b, split_ring)
        far = permute(near, split_ring)
        groups.append([part, b, near, near_other, cross(near), cross(near_other), far])
    return groups


places = ((0, 0, 0), (0, 0, 1), (1, 0, 0), (1, 0, 1), (-1, 0, 1), (-1, 0, 0), (0, 2, 0), (0, 2, 1))


def shards(gradients, left_factor, right_factor, left_root, right_root, owner_table):
    owners = lax.axis_size("fsdp")
    block = left_factor.shape[-1]
    _, row_count, col_count = gradients.shape

    swapped = permute(gradients, core_swap)
    grouped = (8, row_count // 8, col_count)
    own = own_rows(gradients.reshape(grouped))
    sums = pair_sum(own, swapped.reshape(grouped), block)
    kept, to_next, to_far, to_prev = sums
    parts = [kept, permute(to_far, y_shift(2)), permute(to_next, y_shift(1)), permute(to_prev, y_shift(-1))]
    (outgoing,) = place(owner_table, parts, owners, block)
    received = lax.all_to_all(outgoing, "fsdp", split_axis=0, concat_axis=0, tiled=True)
    factors = (left_factor[0, 0], right_factor[0, 0], left_root[0, 0], right_root[0, 0])
    blocks = owners // 4
    low, high = gather(received, SPLIT)
    low.append(cross(low[-1]))
    results = update(0, SPLIT, low, *factors, [])
    high.append(cross(high[-1]))
    left_new, right_new, result = update(SPLIT, blocks - SPLIT, high, *factors, results)
    return (left_new[None, None], right_new[None, None], result[None, None])


def solution(mesh):
    placed = (
        P("replica", "fsdp", None),
        P("fsdp", None, None, "replica", None),
        P("fsdp", None, None, "replica", None),
        P("fsdp", None, None, "replica", None),
        P("fsdp", None, None, None, None),
        P(),
    )
    return jax.shard_map(
        shards,
        mesh=mesh,
        in_specs=placed,
        out_specs=(
            P("fsdp", None, None, "replica", None),
            P("fsdp", None, None, "replica", None),
            P("fsdp", None, None, "replica", None),
        ),
        check_vma=False,
    )
```

```python
import jax
import jax.numpy as jnp
from jax import lax
from jax.experimental import pallas as pl
from jax.experimental.pallas import tpu as pltpu
from jax.sharding import PartitionSpec as P

decay_rate = 0.9
MIB = 1 << 20
SPLIT = 4
VMEM = pl.BlockSpec(memory_space=pltpu.VMEM)
SMEM = pl.BlockSpec(memory_space=pltpu.SMEM)
HBM = pl.BlockSpec(memory_space=pltpu.HBM)

core_swap = [(r, r ^ 1) for r in range(8)]
split_ring = [(r, (r + 2 - 4 * (r % 2)) % 8) for r in range(8)]


def y_shift(d):
    return [(r, (r + 2 * d) % 8) for r in range(8)]


def permute(x, pairs):
    return lax.ppermute(x, "replica", pairs)


def group_of(r, k):
    return 2 * lax.rem(r // 2 + k, 4) + lax.rem(r, 2)


def own_rows_kernel(grads, out, sems):
    copies = [pltpu.make_async_copy(grads.at[group_of(lax.axis_index("replica"), k)], out.at[k], sems.at[k]) for k in range(4)]
    for c in copies:
        c.start()
    for c in copies:
        c.wait()


def own_rows(grads):
    _, rows, cols = grads.shape
    return pl.pallas_call(
        own_rows_kernel,
        in_specs=[HBM],
        out_specs=VMEM,
        out_shape=jax.ShapeDtypeStruct((4, rows, cols), grads.dtype),
        scratch_shapes=[pltpu.SemaphoreType.DMA((4,))],
        compiler_params=pltpu.CompilerParams(vmem_limit_bytes=8 * MIB),
        cost_estimate=pl.CostEstimate(flops=0, bytes_accessed=4 * MIB, transcendentals=0),
        name="own_rows",
    )(grads)


def pair_sum_kernel(own, recv, *outs):
    for k in range(4):
        total = own[k].astype(jnp.float32) + recv[group_of(lax.axis_index("replica"), k)].astype(jnp.float32)
        outs[k][...] = total.astype(own.dtype)


def pair_sum(own, recv, block):
    _, rows, cols = own.shape
    return pl.pallas_call(
        pair_sum_kernel,
        in_specs=[VMEM, VMEM],
        out_specs=[VMEM] * 4,
        out_shape=[jax.ShapeDtypeStruct((rows, cols), own.dtype)] * 4,
        compiler_params=pltpu.CompilerParams(vmem_limit_bytes=8 * MIB),
        cost_estimate=pl.CostEstimate(flops=4 * rows * cols, bytes_accessed=4 * MIB, transcendentals=0),
        name="pair_sum",
    )(own, recv)


def place_kernel(table, *refs):
    halves = len(refs) // 5
    my_row = lax.axis_index("fsdp") // 4
    for h in range(halves):
        a, b, c, d = refs[4 * h : 4 * h + 4]
        out = refs[4 * halves + h]
        width = out.shape[-1]
        out[...] = jnp.zeros_like(out)
        for col in range(a.shape[-1] // width):
            cut = slice(col * width, (col + 1) * width)
            total = (
                a[:, cut].astype(jnp.float32)
                + b[:, cut].astype(jnp.float32)
                + c[:, cut].astype(jnp.float32)
                + d[:, cut].astype(jnp.float32)
            )
            out[table[my_row, col]] = total.astype(out.dtype)


def place(table, parts, owners, width):
    rows, cols = parts[0].shape
    halves = len(parts) // 4
    return pl.pallas_call(
        place_kernel,
        in_specs=[SMEM] + [VMEM] * len(parts),
        out_specs=[VMEM] * halves,
        out_shape=[jax.ShapeDtypeStruct((owners, rows, width), parts[0].dtype)] * halves,
        compiler_params=pltpu.CompilerParams(vmem_limit_bytes=8 * MIB),
        cost_estimate=pl.CostEstimate(flops=4 * rows * cols * halves, bytes_accessed=MIB * halves, transcendentals=0),
        name="place",
    )(table, *parts)


def update_kernel(first, *refs):
    pieces, (left, right, lroot, rroot) = refs[: len(places)], refs[len(places) : len(places) + 4]
    left_out, right_out, out, whole, left_new, right_new, result, sems = refs[-8:]
    r = lax.axis_index("replica")
    y, core = r // 2, lax.rem(r, 2)
    count, share, size = left_new.shape
    quarter = size // 4
    scale = (1.0 - decay_rate) / size
    sends = []
    for n in range(count):
        j = first + n
        block = whole.at[n]
        for piece, (ahead, dy, flip) in zip(pieces, places):
            row = 2 * lax.rem(y + dy + ahead * (2 * core - 1) + 4, 4) + (1 - core if flip else core)
            for q in range(4):
                start = pl.multiple_of(q * quarter + row * 16, 16)
                block[pl.ds(start, 16), :] = piece[4 * n + q]
        mine = block[pl.ds(pl.multiple_of(r * share, share), share), :]
        stat_left = lax.dot_general(block[...], mine, (((1,), (1,)), ((), ())), preferred_element_type=jnp.float32).T
        left_new[n] = decay_rate * left[j] + scale * stat_left
        turned = block[:, pl.ds(pl.multiple_of(y * 2 * share, 2 * share), 2 * share)].T
        turned = jnp.where(core == 0, turned[:share], turned[share:])
        both = jnp.dot(jnp.concatenate([turned, lroot[j]], axis=0), block[...], preferred_element_type=jnp.float32)
        right_new[n] = decay_rate * right[j] + scale * both[:share]
        half = both[share:].astype(jnp.bfloat16)
        result[n] = jnp.dot(half, rroot[j], preferred_element_type=jnp.float32).astype(result.dtype)
        for m, (src, dst) in enumerate(((left_new, left_out), (right_new, right_out), (result, out))):
            sends.append(pltpu.make_async_copy(src.at[n], dst.at[j], sems.at[m, n]))
            sends[-1].start()
    for send in sends:
        send.wait()


def update(first, count, pieces, left, right, lroot, rroot, earlier):
    _, share, size = left.shape
    shapes = [jax.ShapeDtypeStruct(x.shape, x.dtype) for x in (left, right, lroot)]
    return pl.pallas_call(
        lambda *refs: update_kernel(first, *refs),
        in_specs=[VMEM] * (len(pieces) + 4) + [HBM] * len(earlier),
        out_specs=[HBM] * 3,
        out_shape=shapes,
        scratch_shapes=[pltpu.VMEM((count, size, size), lroot.dtype)]
        + [pltpu.VMEM((count, share, size), x.dtype) for x in shapes]
        + [pltpu.SemaphoreType.DMA((3, count))],
        input_output_aliases={len(pieces) + 4 + n: n for n in range(len(earlier))},
        compiler_params=pltpu.CompilerParams(vmem_limit_bytes=16 * MIB),
        cost_estimate=pl.CostEstimate(flops=count * 8 * share * size * size, bytes_accessed=2 * count * MIB, transcendentals=0),
        name="update",
    )(*pieces, left, right, lroot, rroot, *earlier)


def tie(*xs):
    return lax.optimization_barrier(xs)


def cross(x):
    return permute(x, core_swap)


def gather(own, split):
    x, y = own[: 4 * split], own[4 * split :]
    x_near = permute(x, split_ring)
    x_other = cross(x)
    y_tied, _ = tie(y, x_other)
    y_other, y_near = cross(y_tied), permute(y_tied, split_ring)
    x_near_other, y_near_other = permute(x_other, split_ring), permute(y_other, split_ring)
    x_far, y_far = permute(tie(x_near, x_other, y_other)[0], split_ring), permute(tie(y_near, y_other)[0], split_ring)
    groups = []
    for part, other, near, near_other, far in ((x, x_other, x_near, x_near_other, x_far), (y, y_other, y_near, y_near_other, y_far)):
        groups.append([part, other, near, near_other, cross(near), cross(near_other), far])
    return groups


places = ((0, 0, 0), (0, 0, 1), (1, 0, 0), (1, 0, 1), (-1, 0, 1), (-1, 0, 0), (0, 2, 0), (0, 2, 1))


def shards(gradients, left_factor, right_factor, left_root, right_root, owner_table):
    owners = lax.axis_size("fsdp")
    block = left_factor.shape[-1]
    _, row_count, col_count = gradients.shape

    swapped = permute(gradients, core_swap)
    grouped = (8, row_count // 8, col_count)
    own = own_rows(gradients.reshape(grouped))
    sums = pair_sum(own, swapped.reshape(grouped), block)
    kept, to_next, to_far, to_prev = sums
    parts = [kept, permute(to_far, y_shift(2)), permute(to_next, y_shift(1)), permute(to_prev, y_shift(-1))]
    (outgoing,) = place(owner_table, parts, owners, block)
    received = lax.all_to_all(outgoing, "fsdp", split_axis=0, concat_axis=0, tiled=True)
    factors = (left_factor[0, 0], right_factor[0, 0], left_root[0, 0], right_root[0, 0])
    blocks = owners // 4
    low, high = gather(received, SPLIT)
    low.append(cross(low[-1]))
    results = update(0, SPLIT, low, *factors, [])
    high.append(cross(high[-1]))
    left_new, right_new, result = update(SPLIT, blocks - SPLIT, high, *factors, results)
    return (left_new[None, None], right_new[None, None], result[None, None])


def solution(mesh):
    placed = (
        P("replica", "fsdp", None),
        P("fsdp", None, None, "replica", None),
        P("fsdp", None, None, "replica", None),
        P("fsdp", None, None, "replica", None),
        P("fsdp", None, None, None, None),
        P(),
    )
    return jax.shard_map(
        shards,
        mesh=mesh,
        in_specs=placed,
        out_specs=(
            P("fsdp", None, None, "replica", None),
            P("fsdp", None, None, "replica", None),
            P("fsdp", None, None, "replica", None),
        ),
        check_vma=False,
    )
```

```python
import jax
import jax.numpy as jnp
from jax import lax
from jax.experimental import pallas as pl
from jax.experimental.pallas import tpu as pltpu
from jax.sharding import PartitionSpec as P

decay_rate = 0.9
MIB = 1 << 20
SPLIT = 4
VMEM = pl.BlockSpec(memory_space=pltpu.VMEM)
SMEM = pl.BlockSpec(memory_space=pltpu.SMEM)
HBM = pl.BlockSpec(memory_space=pltpu.HBM)

core_swap = [(r, r ^ 1) for r in range(8)]
split_ring = [(r, (r + 2 - 4 * (r % 2)) % 8) for r in range(8)]


def y_shift(d):
    return [(r, (r + 2 * d) % 8) for r in range(8)]


def permute(x, pairs):
    return lax.ppermute(x, "replica", pairs)


def group_of(r, k):
    return 2 * lax.rem(r // 2 + k, 4) + lax.rem(r, 2)


def split_kernel(grads, own, first, second, sems):
    r = lax.axis_index("replica")
    copies = []
    for k in range(4):
        target = (second, first, first, second)[k]
        slot = (1, 1, 0, 0)[k]
        mine = group_of(r, k)
        theirs = mine + 1 - 2 * lax.rem(r, 2)
        copies.append(pltpu.make_async_copy(grads.at[theirs], target.at[slot], sems.at[2 * k]))
        copies.append(pltpu.make_async_copy(grads.at[mine], own.at[k], sems.at[2 * k + 1]))
    for c in copies:
        c.start()
    for c in copies:
        c.wait()


def split(grads):
    _, rows, cols = grads.shape
    return pl.pallas_call(
        split_kernel,
        in_specs=[HBM],
        out_specs=[VMEM] * 3,
        out_shape=[jax.ShapeDtypeStruct((n, rows, cols), grads.dtype) for n in (4, 2, 2)],
        scratch_shapes=[pltpu.SemaphoreType.DMA((8,))],
        compiler_params=pltpu.CompilerParams(vmem_limit_bytes=8 * MIB),
        cost_estimate=pl.CostEstimate(flops=0, bytes_accessed=4 * MIB, transcendentals=0),
        name="split",
    )(grads)


def pair_sum_kernel(groups, own, recv, *outs):
    for n, k in enumerate(groups):
        outs[n][...] = (own[k].astype(jnp.float32) + recv[n].astype(jnp.float32)).astype(own.dtype)


def pair_sum(groups, own, recv, *extra):
    _, rows, cols = own.shape
    return pl.pallas_call(
        lambda own, recv, *refs: pair_sum_kernel(groups, own, recv, *refs[-2:]),
        in_specs=[VMEM, VMEM] + [SMEM] * len(extra),
        out_specs=[VMEM] * 2,
        out_shape=[jax.ShapeDtypeStruct((rows, cols), own.dtype)] * 2,
        compiler_params=pltpu.CompilerParams(vmem_limit_bytes=8 * MIB),
        cost_estimate=pl.CostEstimate(flops=2 * rows * cols, bytes_accessed=2 * MIB, transcendentals=0),
        name="pair_sum",
    )(own, recv, *extra)


def place_kernel(table, *refs):
    halves = len(refs) // 5
    my_row = lax.axis_index("fsdp") // 4
    for h in range(halves):
        a, b, c, d = refs[4 * h : 4 * h + 4]
        out = refs[4 * halves + h]
        width = out.shape[-1]
        out[...] = jnp.zeros_like(out)
        for col in range(a.shape[-1] // width):
            cut = slice(col * width, (col + 1) * width)
            total = (
                a[:, cut].astype(jnp.float32)
                + b[:, cut].astype(jnp.float32)
                + c[:, cut].astype(jnp.float32)
                + d[:, cut].astype(jnp.float32)
            )
            out[table[my_row, col]] = total.astype(out.dtype)


def place(table, parts, owners, width):
    rows, cols = parts[0].shape
    halves = len(parts) // 4
    return pl.pallas_call(
        place_kernel,
        in_specs=[SMEM] + [VMEM] * len(parts),
        out_specs=[VMEM] * halves,
        out_shape=[jax.ShapeDtypeStruct((owners, rows, width), parts[0].dtype)] * halves,
        compiler_params=pltpu.CompilerParams(vmem_limit_bytes=8 * MIB),
        cost_estimate=pl.CostEstimate(flops=4 * rows * cols * halves, bytes_accessed=MIB * halves, transcendentals=0),
        name="place",
    )(table, *parts)


def update_kernel(first, *refs):
    pieces, (left, right, lroot, rroot) = refs[: len(places)], refs[len(places) : len(places) + 4]
    left_out, right_out, out, whole, left_new, right_new, result, sems = refs[-8:]
    r = lax.axis_index("replica")
    y, core = r // 2, lax.rem(r, 2)
    count, share, size = left_new.shape
    quarter = size // 4
    scale = (1.0 - decay_rate) / size
    sends = []
    for n in range(count):
        j = first + n
        block = whole.at[n]
        for piece, (ahead, dy, flip) in zip(pieces, places):
            row = 2 * lax.rem(y + dy + ahead * (2 * core - 1) + 4, 4) + (1 - core if flip else core)
            for q in range(4):
                start = pl.multiple_of(q * quarter + row * 16, 16)
                block[pl.ds(start, 16), :] = piece[4 * n + q]
        mine = block[pl.ds(pl.multiple_of(r * share, share), share), :]
        stat_left = lax.dot_general(block[...], mine, (((1,), (1,)), ((), ())), preferred_element_type=jnp.float32).T
        left_new[n] = decay_rate * left[j] + scale * stat_left
        turned = block[:, pl.ds(pl.multiple_of(y * 2 * share, 2 * share), 2 * share)].T
        turned = jnp.where(core == 0, turned[:share], turned[share:])
        both = jnp.dot(jnp.concatenate([turned, lroot[j]], axis=0), block[...], preferred_element_type=jnp.float32)
        right_new[n] = decay_rate * right[j] + scale * both[:share]
        half = both[share:].astype(jnp.bfloat16)
        result[n] = jnp.dot(half, rroot[j], preferred_element_type=jnp.float32).astype(result.dtype)
        for m, (src, dst) in enumerate(((left_new, left_out), (right_new, right_out), (result, out))):
            sends.append(pltpu.make_async_copy(src.at[n], dst.at[j], sems.at[m, n]))
            sends[-1].start()
    for send in sends:
        send.wait()


def update(first, count, pieces, left, right, lroot, rroot, earlier):
    _, share, size = left.shape
    shapes = [jax.ShapeDtypeStruct(x.shape, x.dtype) for x in (left, right, lroot)]
    return pl.pallas_call(
        lambda *refs: update_kernel(first, *refs),
        in_specs=[VMEM] * (len(pieces) + 4) + [HBM] * len(earlier),
        out_specs=[HBM] * 3,
        out_shape=shapes,
        scratch_shapes=[pltpu.VMEM((count, size, size), lroot.dtype)]
        + [pltpu.VMEM((count, share, size), x.dtype) for x in shapes]
        + [pltpu.SemaphoreType.DMA((3, count))],
        input_output_aliases={len(pieces) + 4 + n: n for n in range(len(earlier))},
        compiler_params=pltpu.CompilerParams(vmem_limit_bytes=16 * MIB),
        cost_estimate=pl.CostEstimate(flops=count * 8 * share * size * size, bytes_accessed=2 * count * MIB, transcendentals=0),
        name="update",
    )(*pieces, left, right, lroot, rroot, *earlier)


def tie(*xs):
    return lax.optimization_barrier(xs)


def cross(x):
    return permute(x, core_swap)


def gather(own, split):
    x, y = own[: 4 * split], own[4 * split :]
    x_near = permute(x, split_ring)
    x_other = cross(x)
    y_tied, _ = tie(y, x_other)
    y_other, y_near = cross(y_tied), permute(y_tied, split_ring)
    x_near_other, y_near_other = permute(x_other, split_ring), permute(y_other, split_ring)
    x_far, y_far = permute(tie(x_near, x_other, y_other)[0], split_ring), permute(tie(y_near, y_other)[0], split_ring)
    groups = []
    for part, other, near, near_other, far in ((x, x_other, x_near, x_near_other, x_far), (y, y_other, y_near, y_near_other, y_far)):
        groups.append([part, other, near, near_other, cross(near), cross(near_other), far])
    return groups


places = ((0, 0, 0), (0, 0, 1), (1, 0, 0), (1, 0, 1), (-1, 0, 1), (-1, 0, 0), (0, 2, 0), (0, 2, 1))


def shards(gradients, left_factor, right_factor, left_root, right_root, owner_table):
    owners = lax.axis_size("fsdp")
    block = left_factor.shape[-1]
    _, row_count, col_count = gradients.shape

    own, first, second = split(gradients.reshape(8, row_count // 8, col_count))
    first = cross(first)
    to_far, to_next = pair_sum((2, 1), own, first)
    second, _ = tie(second, first)
    to_prev, kept = pair_sum((3, 0), own, cross(second), owner_table)
    parts = [kept, permute(to_far, y_shift(2)), permute(to_next, y_shift(1)), permute(to_prev, y_shift(-1))]
    (outgoing,) = place(owner_table, parts, owners, block)
    received = lax.all_to_all(outgoing, "fsdp", split_axis=0, concat_axis=0, tiled=True)
    factors = (left_factor[0, 0], right_factor[0, 0], left_root[0, 0], right_root[0, 0])
    blocks = owners // 4
    low, high = gather(received, SPLIT)
    low.append(cross(low[-1]))
    results = update(0, SPLIT, low, *factors, [])
    high.append(cross(high[-1]))
    left_new, right_new, result = update(SPLIT, blocks - SPLIT, high, *factors, results)
    return (left_new[None, None], right_new[None, None], result[None, None])


def solution(mesh):
    placed = (
        P("replica", "fsdp", None),
        P("fsdp", None, None, "replica", None),
        P("fsdp", None, None, "replica", None),
        P("fsdp", None, None, "replica", None),
        P("fsdp", None, None, None, None),
        P(),
    )
    return jax.shard_map(
        shards,
        mesh=mesh,
        in_specs=placed,
        out_specs=(
            P("fsdp", None, None, "replica", None),
            P("fsdp", None, None, "replica", None),
            P("fsdp", None, None, "replica", None),
        ),
        check_vma=False,
    )
```

```python
import jax
import jax.numpy as jnp
from jax import lax
from jax.experimental import pallas as pl
from jax.experimental.pallas import tpu as pltpu
from jax.sharding import PartitionSpec as P

decay_rate = 0.9
MIB = 1 << 20
SPLIT = 4
VMEM = pl.BlockSpec(memory_space=pltpu.VMEM)
SMEM = pl.BlockSpec(memory_space=pltpu.SMEM)
HBM = pl.BlockSpec(memory_space=pltpu.HBM)

core_swap = [(r, r ^ 1) for r in range(8)]
split_ring = [(r, (r + 2 - 4 * (r % 2)) % 8) for r in range(8)]


def y_shift(d):
    return [(r, (r + 2 * d) % 8) for r in range(8)]


def permute(x, pairs):
    return lax.ppermute(x, "replica", pairs)


def group_of(r, k):
    return 2 * lax.rem(r // 2 + k, 4) + lax.rem(r, 2)


def split_kernel(grads, own, first, second, sems):
    r = lax.axis_index("replica")
    copies = []
    for k in range(4):
        target = (second, first, first, second)[k]
        slot = (1, 1, 0, 0)[k]
        mine = group_of(r, k)
        theirs = mine + 1 - 2 * lax.rem(r, 2)
        copies.append(pltpu.make_async_copy(grads.at[theirs], target.at[slot], sems.at[2 * k]))
        copies.append(pltpu.make_async_copy(grads.at[mine], own.at[k], sems.at[2 * k + 1]))
    for c in copies:
        c.start()
    for c in copies:
        c.wait()


def split(grads):
    _, rows, cols = grads.shape
    return pl.pallas_call(
        split_kernel,
        in_specs=[HBM],
        out_specs=[VMEM] * 3,
        out_shape=[jax.ShapeDtypeStruct((n, rows, cols), grads.dtype) for n in (4, 2, 2)],
        scratch_shapes=[pltpu.SemaphoreType.DMA((8,))],
        compiler_params=pltpu.CompilerParams(vmem_limit_bytes=8 * MIB),
        cost_estimate=pl.CostEstimate(flops=0, bytes_accessed=4 * MIB, transcendentals=0),
        name="split",
    )(grads)


def pair_sum_kernel(groups, own, recv, *outs):
    for out, (k, n) in zip(outs, groups):
        out[...] = (own[k].astype(jnp.float32) + recv[n].astype(jnp.float32)).astype(own.dtype)


def pair_sum(groups, own, recv, *extra):
    _, rows, cols = own.shape
    return pl.pallas_call(
        lambda own, recv, *refs: pair_sum_kernel(groups, own, recv, *refs[-len(groups) :]),
        in_specs=[VMEM, VMEM] + [SMEM] * len(extra),
        out_specs=[VMEM] * len(groups),
        out_shape=[jax.ShapeDtypeStruct((rows, cols), own.dtype)] * len(groups),
        compiler_params=pltpu.CompilerParams(vmem_limit_bytes=8 * MIB),
        cost_estimate=pl.CostEstimate(flops=len(groups) * rows * cols, bytes_accessed=len(groups) * MIB, transcendentals=0),
        name="pair_sum",
    )(own, recv, *extra)


def place_kernel(table, *refs):
    halves = len(refs) // 5
    my_row = lax.axis_index("fsdp") // 4
    for h in range(halves):
        a, b, c, d = refs[4 * h : 4 * h + 4]
        out = refs[4 * halves + h]
        width = out.shape[-1]
        out[...] = jnp.zeros_like(out)
        for col in range(a.shape[-1] // width):
            cut = slice(col * width, (col + 1) * width)
            total = (
                a[:, cut].astype(jnp.float32)
                + b[:, cut].astype(jnp.float32)
                + c[:, cut].astype(jnp.float32)
                + d[:, cut].astype(jnp.float32)
            )
            out[table[my_row, col]] = total.astype(out.dtype)


def place(table, parts, owners, width):
    rows, cols = parts[0].shape
    halves = len(parts) // 4
    return pl.pallas_call(
        place_kernel,
        in_specs=[SMEM] + [VMEM] * len(parts),
        out_specs=[VMEM] * halves,
        out_shape=[jax.ShapeDtypeStruct((owners, rows, width), parts[0].dtype)] * halves,
        compiler_params=pltpu.CompilerParams(vmem_limit_bytes=8 * MIB),
        cost_estimate=pl.CostEstimate(flops=4 * rows * cols * halves, bytes_accessed=MIB * halves, transcendentals=0),
        name="place",
    )(table, *parts)


def update_kernel(first, *refs):
    pieces, (left, right, lroot, rroot) = refs[: len(places)], refs[len(places) : len(places) + 4]
    left_out, right_out, out, whole, left_new, right_new, result, sems = refs[-8:]
    r = lax.axis_index("replica")
    y, core = r // 2, lax.rem(r, 2)
    count, share, size = left_new.shape
    quarter = size // 4
    scale = (1.0 - decay_rate) / size
    sends = []
    for n in range(count):
        j = first + n
        block = whole.at[n]
        for piece, (ahead, dy, flip) in zip(pieces, places):
            row = 2 * lax.rem(y + dy + ahead * (2 * core - 1) + 4, 4) + (1 - core if flip else core)
            for q in range(4):
                start = pl.multiple_of(q * quarter + row * 16, 16)
                block[pl.ds(start, 16), :] = piece[4 * n + q]
        mine = block[pl.ds(pl.multiple_of(r * share, share), share), :]
        stat_left = lax.dot_general(block[...], mine, (((1,), (1,)), ((), ())), preferred_element_type=jnp.float32).T
        left_new[n] = decay_rate * left[j] + scale * stat_left
        turned = block[:, pl.ds(pl.multiple_of(y * 2 * share, 2 * share), 2 * share)].T
        turned = jnp.where(core == 0, turned[:share], turned[share:])
        both = jnp.dot(jnp.concatenate([turned, lroot[j]], axis=0), block[...], preferred_element_type=jnp.float32)
        right_new[n] = decay_rate * right[j] + scale * both[:share]
        half = both[share:].astype(jnp.bfloat16)
        result[n] = jnp.dot(half, rroot[j], preferred_element_type=jnp.float32).astype(result.dtype)
        for m, (src, dst) in enumerate(((left_new, left_out), (right_new, right_out), (result, out))):
            sends.append(pltpu.make_async_copy(src.at[n], dst.at[j], sems.at[m, n]))
            sends[-1].start()
    for send in sends:
        send.wait()


def update(first, count, pieces, left, right, lroot, rroot, earlier):
    _, share, size = left.shape
    shapes = [jax.ShapeDtypeStruct(x.shape, x.dtype) for x in (left, right, lroot)]
    return pl.pallas_call(
        lambda *refs: update_kernel(first, *refs),
        in_specs=[VMEM] * (len(pieces) + 4) + [HBM] * len(earlier),
        out_specs=[HBM] * 3,
        out_shape=shapes,
        scratch_shapes=[pltpu.VMEM((count, size, size), lroot.dtype)]
        + [pltpu.VMEM((count, share, size), x.dtype) for x in shapes]
        + [pltpu.SemaphoreType.DMA((3, count))],
        input_output_aliases={len(pieces) + 4 + n: n for n in range(len(earlier))},
        compiler_params=pltpu.CompilerParams(vmem_limit_bytes=16 * MIB),
        cost_estimate=pl.CostEstimate(flops=count * 8 * share * size * size, bytes_accessed=2 * count * MIB, transcendentals=0),
        name="update",
    )(*pieces, left, right, lroot, rroot, *earlier)


def tie(*xs):
    return lax.optimization_barrier(xs)


def cross(x):
    return permute(x, core_swap)


def gather(own, split):
    x, y = own[: 4 * split], own[4 * split :]
    x_near = permute(x, split_ring)
    x_other = cross(x)
    y_tied, _ = tie(y, x_other)
    y_other, y_near = cross(y_tied), permute(y_tied, split_ring)
    x_near_other, y_near_other = permute(x_other, split_ring), permute(y_other, split_ring)
    x_far, y_far = permute(tie(x_near, x_other, y_other)[0], split_ring), permute(tie(y_near, y_other)[0], split_ring)
    groups = []
    for part, other, near, near_other, far in ((x, x_other, x_near, x_near_other, x_far), (y, y_other, y_near, y_near_other, y_far)):
        groups.append([part, other, near, near_other, cross(near), cross(near_other), far])
    return groups


places = ((0, 0, 0), (0, 0, 1), (1, 0, 0), (1, 0, 1), (-1, 0, 1), (-1, 0, 0), (0, 2, 0), (0, 2, 1))


def shards(gradients, left_factor, right_factor, left_root, right_root, owner_table):
    owners = lax.axis_size("fsdp")
    block = left_factor.shape[-1]
    _, row_count, col_count = gradients.shape

    own, first, second = split(gradients.reshape(8, row_count // 8, col_count))
    first = cross(first)
    to_far, to_next = pair_sum(((2, 0), (1, 1)), own, first)
    second, _ = tie(second, first)
    second = cross(second)
    (to_prev,) = pair_sum(((3, 0),), own, second)
    (kept,) = pair_sum(((0, 1),), own, second, owner_table)
    parts = [kept, permute(to_far, y_shift(2)), permute(to_next, y_shift(1)), permute(to_prev, y_shift(-1))]
    (outgoing,) = place(owner_table, parts, owners, block)
    received = lax.all_to_all(outgoing, "fsdp", split_axis=0, concat_axis=0, tiled=True)
    factors = (left_factor[0, 0], right_factor[0, 0], left_root[0, 0], right_root[0, 0])
    blocks = owners // 4
    low, high = gather(received, SPLIT)
    low.append(cross(low[-1]))
    results = update(0, SPLIT, low, *factors, [])
    high.append(cross(high[-1]))
    left_new, right_new, result = update(SPLIT, blocks - SPLIT, high, *factors, results)
    return (left_new[None, None], right_new[None, None], result[None, None])


def solution(mesh):
    placed = (
        P("replica", "fsdp", None),
        P("fsdp", None, None, "replica", None),
        P("fsdp", None, None, "replica", None),
        P("fsdp", None, None, "replica", None),
        P("fsdp", None, None, None, None),
        P(),
    )
    return jax.shard_map(
        shards,
        mesh=mesh,
        in_specs=placed,
        out_specs=(
            P("fsdp", None, None, "replica", None),
            P("fsdp", None, None, "replica", None),
            P("fsdp", None, None, "replica", None),
        ),
        check_vma=False,
    )
```
